32 devices in a mesh: scene: 2 (over y), ctx: 4 (over x, core), head: 4 (over z).
Axes of the slice: x: 2, y: 2, z: 4, core: 2. Of those that a mesh axis runs over, the one named last changes fastest.
Arguments:
- frames_in: float32 [8192, 1024], P(('scene', 'ctx')), parts along dimension 0, may hold values from -6 to 6
- merge_index: int32 [8192], P(('scene', 'ctx')), parts along dimension 0, may hold values from 0 to 1023, as said below
- frame_query: float32 [1024, 1024], P(None, 'head'), may hold values from -1 to 1
- frame_key: float32 [1024, 1024], P(None, 'head'), may hold values from -1 to 1
- frame_value: float32 [1024, 1024], P(None, 'head'), may hold values from -0.1875 to 0.1875
- frame_out: float32 [1024, 1024], P('head'), may hold values from -0.1875 to 0.1875
- global_query: float32 [1024, 1024], P(None, 'head'), may hold values from -1 to 1
- global_key: float32 [1024, 1024], P(None, 'head'), may hold values from -1 to 1
- global_value: float32 [1024, 1024], P(None, 'head'), may hold values from -0.1875 to 0.1875
- global_out: float32 [1024, 1024], P('head'), may hold values from -0.1875 to 0.1875
Outputs:
- refined: float32 [8192, 1024], P(('scene', 'ctx'), 'head'), parts along dimension 0
- merged_tokens: float32 [2048, 1024], P(('scene', 'ctx'), 'head'), parts along dimension 0
The draws below stay inside these ranges and needn't reach their ends.
There are 2 independent parts, one for each index of `scene`. The reference program is written for one: setup_inputs(seed, part) draws one part's arguments, and reference() takes and returns one part's arrays. A program takes and returns all parts, laid end to end along the dimension named above; an argument that names none is the same for every part. Nothing has to cross between parts.
Inputs may be any that keep to these rules, and one draw needn't show every extreme that they name: `merge_index`: each of the 1024 merged tokens is named by at least one patch; merged tokens i * 256 to (i + 1) * 256 - 1 belong to index i of ctx; of the 1024 patches of one index of ctx at most 512 name merged tokens of any one index of ctx, exactly 512 for some index; the merged tokens of each index of ctx are named by exactly 1024 patches in all.
All inputs are finite; a program needn't handle non-finite values.
Results may differ from the reference program's by a relative error of at most 0.0003.
Values sent between devices are 32-bit elements; how exact they have to be, the bound alone decides.
A program may use at most 64 MiB of HBM per device.

```python
import jax
import jax.numpy as jnp
from jax import lax

D = 1024
HEADS = 16
HEAD_DIM = 64
PATCHES = 256
TOK_DEV = 1024
MERGE_DEV = 256
FRAMES = 16
TOKENS = 4096
MERGED = 1024


def paired_maps(key, salt):
    base = jax.random.fold_in(key, salt)
    first = jax.random.normal(jax.random.fold_in(base, 2), (D, D), jnp.float32)
    second = jax.random.normal(jax.random.fold_in(base, 3), (D, D), jnp.float32)
    scale_factor = D ** (-0.5)
    return (jnp.clip(first * scale_factor, -1.0, 1.0), jnp.clip(second * scale_factor, -1.0, 1.0))


def draw_frames_in(key, part):
    entries = jax.random.normal(jax.random.fold_in(key, 1), (TOKENS, D), jnp.float32)
    return jnp.clip(entries, -6.0, 6.0)


def draw_merge_index(key, part):
    group_count = TOKENS // TOK_DEV
    mean_load = TOK_DEV // group_count
    pair_order = jax.random.permutation(jax.random.fold_in(key, 1), group_count)
    shift_sizes = jax.random.randint(jax.random.fold_in(key, 2), (group_count // 2,), 0, mean_load + 1, dtype=jnp.int32)
    shift_sizes = shift_sizes.at[0].set(mean_load)
    deltas = jnp.zeros((group_count,), jnp.int32).at[pair_order[0::2]].set(shift_sizes).at[pair_order[1::2]].set(-shift_sizes)
    sender_col = jnp.arange(group_count, dtype=jnp.int32)[:, None]
    owner_row = jnp.arange(group_count, dtype=jnp.int32)[None, :]
    load_table = mean_load + deltas[(owner_row - sender_col) % group_count]
    run_ends = jnp.cumsum(load_table, axis=1)
    run_starts = run_ends - load_table
    before_table = jnp.cumsum(load_table, axis=0) - load_table
    positions = jnp.arange(TOK_DEV, dtype=jnp.int32)
    owner_of = jnp.sum((run_ends[:, None, :] <= positions[None, :, None]).astype(jnp.int32), axis=2)
    within = positions[None, :] - jnp.take_along_axis(run_starts, owner_of, axis=1)
    global_rank = jnp.take_along_axis(before_table, owner_of, axis=1) + within
    label_keys = jax.random.split(jax.random.fold_in(key, 3), group_count)
    label_perms = jax.vmap(lambda one_key: jax.random.permutation(one_key, TOK_DEV))(label_keys)
    extra_labels = jax.random.randint(jax.random.fold_in(key, 4), (group_count, TOK_DEV - MERGE_DEV), 0, MERGE_DEV, dtype=jnp.int32)
    base_labels = jnp.concatenate([jnp.broadcast_to(jnp.arange(MERGE_DEV, dtype=jnp.int32)[None, :], (group_count, MERGE_DEV)), extra_labels], axis=1)
    owner_labels = jnp.take_along_axis(base_labels, label_perms.astype(jnp.int32), axis=1)
    flat_labels = owner_labels.reshape(-1)
    local_label = flat_labels[owner_of * TOK_DEV + global_rank]
    merged_ids = owner_of * MERGE_DEV + local_label
    place_keys = jax.random.split(jax.random.fold_in(key, 5), group_count)
    place_perms = jax.vmap(lambda one_key: jax.random.permutation(one_key, TOK_DEV))(place_keys)
    placed = jnp.take_along_axis(merged_ids, place_perms.astype(jnp.int32), axis=1)
    return placed.reshape(TOKENS).astype(jnp.int32)


def draw_frame_query(key, part):
    return paired_maps(key, 11)[0]


def draw_frame_key(key, part):
    return paired_maps(key, 11)[1]


def draw_global_query(key, part):
    return paired_maps(key, 23)[0]


def draw_global_key(key, part):
    return paired_maps(key, 23)[1]


def shard_levels(own_key, shape, cuts, smallest, largest):
    factor_of = 1.0
    for position, blocks in cuts:
        draws = jax.random.uniform(jax.random.fold_in(jax.random.fold_in(own_key, 6), position), (blocks,), jnp.float32, smallest / len(cuts), largest / len(cuts))
        factor_of = factor_of * jnp.repeat(jnp.exp(draws), shape[position] // blocks).reshape((-1,) + (1,) * (len(shape) - 1 - position))
    return factor_of


def bell_draw(own_key, extent, width, bound, cuts=(), kind=jnp.bfloat16):
    loudness = shard_levels(own_key, extent, cuts, -0.22, 0.18) if cuts else 1.0
    result = jax.random.normal(own_key, extent, jnp.float32) * width * loudness
    return jnp.minimum(jnp.maximum(result, -bound), bound).astype(kind)


def setup_inputs(seed: int = 0, part: int = 0) -> dict:
    keys = jax.random.split(jax.random.key(seed), 11)
    own_keys = jax.random.split(jax.random.fold_in(keys[10], part), 11)
    return {
        "frames_in": draw_frames_in(jax.random.fold_in(jax.random.fold_in(keys[10], part), 71), part),
        "merge_index": draw_merge_index(jax.random.fold_in(jax.random.fold_in(keys[10], part), 71), part),
        "frame_query": draw_frame_query(jax.random.fold_in(keys[10], 71), part),
        "frame_key": draw_frame_key(jax.random.fold_in(keys[10], 71), part),
        "frame_value": bell_draw(keys[4], (D, D), D ** -0.5, 0.1875, ((1, 4),), jnp.float32),
        "frame_out": bell_draw(keys[5], (D, D), D ** -0.5, 0.1875, ((0, 4),), jnp.float32),
        "global_query": draw_global_query(jax.random.fold_in(keys[10], 71), part),
        "global_key": draw_global_key(jax.random.fold_in(keys[10], 71), part),
        "global_value": bell_draw(keys[8], (D, D), D ** -0.5, 0.1875, ((1, 4),), jnp.float32),
        "global_out": bell_draw(keys[9], (D, D), D ** -0.5, 0.1875, ((0, 4),), jnp.float32),
    }


exact_precision = lax.Precision.HIGHEST

def layer_norm(entries):
    center = entries - lax.optimization_barrier(jnp.mean(entries, axis=-1, keepdims=True))
    spread = lax.optimization_barrier(jnp.mean(center * center, axis=-1, keepdims=True))
    return center * lax.rsqrt(spread + 1e-06)

def product(left_side, right_side):
    return jnp.dot(left_side, right_side, precision=exact_precision, preferred_element_type=jnp.float32)

def attend(query_rows, key_rows, value_rows):
    scores = jnp.einsum('qhd,khd->hqk', query_rows, key_rows, precision=exact_precision) * HEAD_DIM ** (-0.5)
    weights = jax.nn.softmax(scores, axis=-1)
    return jnp.einsum('hqk,khd->qhd', weights, value_rows, precision=exact_precision)

def reference(frames_in, merge_index, frame_query, frame_key, frame_value, frame_out, global_query, global_key, global_value, global_out):
    normed = layer_norm(frames_in)

    def one_frame(frame_block):
        query_rows = product(frame_block, frame_query).reshape(PATCHES, HEADS, HEAD_DIM)
        key_rows = product(frame_block, frame_key).reshape(PATCHES, HEADS, HEAD_DIM)
        value_rows = product(frame_block, frame_value).reshape(PATCHES, HEADS, HEAD_DIM)
        return attend(query_rows, key_rows, value_rows).reshape(PATCHES, D)
    attended = lax.map(one_frame, normed.reshape(FRAMES, PATCHES, D)).reshape(TOKENS, D)
    states = frames_in + product(attended, frame_out)
    counts = jax.ops.segment_sum(jnp.ones((TOKENS,), jnp.float32), merge_index, MERGED)
    summed = jax.ops.segment_sum(states, merge_index, MERGED)
    merged = summed / counts[:, None]
    global_normed = layer_norm(merged)
    query_all = product(global_normed, global_query).reshape(MERGED, HEADS, HEAD_DIM).transpose(1, 0, 2)
    key_all = product(global_normed, global_key).reshape(MERGED, HEADS, HEAD_DIM).transpose(1, 0, 2)
    value_all = product(global_normed, global_value).reshape(MERGED, HEADS, HEAD_DIM).transpose(1, 0, 2)

    def one_head(triple):
        scores = product(triple[0], triple[1].T) * HEAD_DIM ** (-0.5)
        weights = jax.nn.softmax(scores, axis=-1)
        return product(weights, triple[2])
    global_attended = lax.map(one_head, (query_all, key_all, value_all)).transpose(1, 0, 2).reshape(MERGED, D)
    update = product(global_attended, global_out)
    merged_tokens = merged + update
    refined = states + update[merge_index]
    return (refined, merged_tokens)
```

```python
import jax
import jax.numpy as jnp
from jax import lax
from jax.sharding import PartitionSpec as P

HEAD_DIM = 64
PATCHES = 256

split_precision = lax.Precision.HIGH


def layer_norm(entries):
    center = entries - jnp.mean(entries, axis=-1, keepdims=True)
    spread = jnp.mean(center * center, axis=-1, keepdims=True)
    return center * lax.rsqrt(spread + 1e-06)


def product(left_side, right_side):
    return jnp.dot(
        left_side, right_side, precision=split_precision, preferred_element_type=jnp.float32
    )


def send_by(block, axis, shift):
    size = lax.axis_size(axis)
    return lax.ppermute(block, axis, [(i, (i + shift) % size) for i in range(size)])


def exchange(piece, axis):
    size = lax.axis_size(axis)
    me = lax.axis_index(axis)
    got = [(me, piece(me))]
    for shift in range(1, size):
        got.append(((me - shift) % size, send_by(piece((me + shift) % size), axis, shift)))
    return got


def place(got, axis_dim, step, count):
    first = got[0][1]
    shape = list(first.shape)
    shape[axis_dim] = step * count
    out = jnp.zeros(shape, first.dtype)
    for source, block in got:
        out = lax.dynamic_update_slice_in_dim(out, block, source * step, axis_dim)
    return out


def gather_ctx(block):
    size = lax.axis_size("ctx")
    me = lax.axis_index("ctx")
    if size % 2:
        got = exchange(lambda d: block, "ctx")
        return jnp.concatenate([b for _, b in got]), [s for s, _ in got]
    owners, blocks = [me], [block]
    for shift in range(2, size, 2):
        blocks.append(send_by(block, "ctx", shift))
        owners.append((me - shift) % size)
    mine = jnp.concatenate(blocks)
    other = lax.ppermute(mine, "ctx", [(i, i ^ 1) for i in range(size)])
    return jnp.concatenate([mine, other]), owners + [o + 1 - 2 * (o % 2) for o in owners]


def per_device(
    frames_in,
    merge_index,
    frame_query,
    frame_key,
    frame_value,
    frame_out,
    global_query,
    global_key,
    global_value,
    global_out,
):
    token_rows = frames_in.shape[0]
    width = frames_in.shape[1]
    local_width = frame_query.shape[1]
    heads_local = local_width // HEAD_DIM
    frame_count = token_rows // PATCHES
    merged_rows = token_rows // 4
    score_scale = HEAD_DIM ** (-0.5)
    ctx_size = lax.axis_size("ctx")
    head_size = lax.axis_size("head")
    scene_size = lax.axis_size("scene")
    ctx_index = lax.axis_index("ctx")
    head_index = lax.axis_index("head")
    head_rows = token_rows // head_size

    peers = scene_size * ctx_size
    share = local_width // peers
    peer = lax.axis_index("scene") * ctx_size + ctx_index
    out_part = lax.dynamic_slice_in_dim(frame_out, peer * share, share, 0)
    out_part = lax.all_gather(out_part, "head", axis=0)
    out_all = lax.all_gather(out_part, ("scene", "ctx"), axis=0)
    out_all = out_all.transpose(1, 0, 2, 3).reshape(head_size * local_width, width)

    index_all = [block for _, block in exchange(lambda d: merge_index, "ctx")]
    owned_ids = ctx_index * merged_rows + jnp.arange(merged_rows, dtype=jnp.int32)
    counts = sum(
        jnp.sum((owned_ids[:, None] == block[None, :]).astype(jnp.float32), axis=1)
        for block in index_all
    )
    merged_ids = jnp.arange(merged_rows * ctx_size, dtype=jnp.int32)
    table = (merged_ids[:, None] == merge_index[None, :]).astype(jnp.bfloat16)

    def merge_sum(rows):
        high = lax.reduce_precision(rows, 8, 7)
        low = rows - high
        pair = jnp.concatenate([high.astype(jnp.bfloat16), low.astype(jnp.bfloat16)], axis=1)
        both = jnp.dot(table, pair, preferred_element_type=jnp.float32)
        both = both[:, : rows.shape[1]] + both[:, rows.shape[1] :]
        got = exchange(
            lambda d: lax.dynamic_slice_in_dim(both, d * merged_rows, merged_rows, 0), "ctx"
        )
        return sum(block for _, block in got)

    def gather_features(block):
        return place(exchange(lambda d: block, "head"), 1, local_width, head_size)

    feature_slice = lax.dynamic_slice_in_dim(frames_in, head_index * local_width, local_width, 1)
    frames_sum = gather_features(merge_sum(feature_slice))

    normed = layer_norm(frames_in)
    query_rows = product(normed, frame_query).reshape(frame_count, PATCHES, heads_local, HEAD_DIM)
    key_rows = product(normed, frame_key).reshape(frame_count, PATCHES, heads_local, HEAD_DIM)
    value_rows = product(normed, frame_value).reshape(frame_count, PATCHES, heads_local, HEAD_DIM)
    scores = (
        jnp.einsum("fqhd,fkhd->fhqk", query_rows, key_rows, precision=split_precision) * score_scale
    )
    weights = jax.nn.softmax(scores, axis=-1)
    attended = jnp.einsum(
        "fhqk,fkhd->fqhd", weights, value_rows, precision=split_precision
    ).reshape(token_rows, local_width)

    attended_sum = gather_features(merge_sum(attended))
    full_merged = (frames_sum + product(attended_sum, out_all)) / counts[:, None]
    merged = lax.dynamic_slice_in_dim(full_merged, head_index * local_width, local_width, 1)

    row_part = place(
        exchange(
            lambda d: lax.dynamic_slice_in_dim(attended, d * head_rows, head_rows, 0), "head"
        ),
        1,
        local_width,
        head_size,
    )
    row_part = product(row_part, out_all)
    states = feature_slice + place(
        exchange(
            lambda d: lax.dynamic_slice_in_dim(row_part, d * local_width, local_width, 1), "head"
        ),
        0,
        head_rows,
        head_size,
    )

    global_normed = layer_norm(full_merged)
    global_k = product(global_normed, global_key)
    global_v = product(global_normed, global_value)
    key_value, _ = gather_ctx(jnp.concatenate([global_k, global_v], axis=1))
    global_q = product(global_normed, global_query).reshape(merged_rows, heads_local, HEAD_DIM)
    key_block = key_value[:, :local_width].reshape(-1, heads_local, HEAD_DIM)
    value_block = key_value[:, local_width:].reshape(-1, heads_local, HEAD_DIM)
    block_scores = (
        jnp.einsum("qhd,khd->hqk", global_q, key_block, precision=split_precision) * score_scale
    )
    block_weights = jnp.exp(block_scores - jnp.max(block_scores, axis=-1, keepdims=True))
    denominator = jnp.sum(block_weights, axis=-1)
    accumulated = jnp.einsum("hqk,khd->hqd", block_weights, value_block, precision=split_precision)
    global_attended = (
        (accumulated / denominator[..., None]).transpose(1, 0, 2).reshape(merged_rows, local_width)
    )
    update_part = product(global_attended, global_out)
    update = sum(
        block
        for _, block in exchange(
            lambda d: lax.dynamic_slice_in_dim(update_part, d * local_width, local_width, 1),
            "head",
        )
    )
    merged_tokens = merged + update
    portion, owners = gather_ctx(update)
    slot_ids = jnp.concatenate(
        [o * merged_rows + jnp.arange(merged_rows, dtype=jnp.int32) for o in owners]
    )
    spread_table = (merge_index[:, None] == slot_ids[None, :]).astype(jnp.float32)
    refined = states + product(spread_table, portion)
    return (refined, merged_tokens)


def solution(mesh):
    placed = (
        P(("scene", "ctx"), None),
        P(("scene", "ctx")),
        P(None, "head"),
        P(None, "head"),
        P(None, "head"),
        P("head", None),
        P(None, "head"),
        P(None, "head"),
        P(None, "head"),
        P("head", None),
    )
    return jax.shard_map(
        per_device,
        mesh=mesh,
        in_specs=placed,
        out_specs=(P(("scene", "ctx"), "head"), P(("scene", "ctx"), "head")),
        check_vma=False,
    )
```

```python
import functools

import jax
import jax.numpy as jnp
from jax import lax
from jax.experimental import pallas as pl
from jax.experimental.pallas import tpu as pltpu
from jax.sharding import PartitionSpec as P

HEAD_DIM = 64
PATCHES = 256
MESH = pl.DeviceIdType.MESH


def split(x):
    high = x.astype(jnp.bfloat16)
    return high, (x - high.astype(jnp.float32)).astype(jnp.bfloat16)


def dot(a, b, contract=((1,), (0,))):
    return lax.dot_general(a, b, (contract, ((), ())), preferred_element_type=jnp.float32)


def dot3(a, b, contract=((1,), (0,))):
    (a_high, a_low), (b_high, b_low) = a, b
    return (
        dot(a_high, b_high, contract) + dot(a_high, b_low, contract) + dot(a_low, b_high, contract)
    )


def layer_norm(entries):
    center = entries - jnp.mean(entries, axis=-1, keepdims=True)
    spread = jnp.mean(center * center, axis=-1, keepdims=True)
    return center * lax.rsqrt(spread + 1e-06)


def attend(query, key, value):
    scores = dot3(split(query * HEAD_DIM ** (-0.5)), split(key), ((1,), (1,)))
    weights = jnp.exp(scores - jnp.max(scores, axis=-1, keepdims=True))
    total = jnp.sum(weights, axis=-1, keepdims=True)
    return dot3(split(weights), split(value)) / total


def kernel(
    n, m,
    frames, index_row, index_col, fq, fk, fv, fo, gq, gk, gv, go,
    refined, merged_tokens,
    fw_high, fw_low, gw_high, gw_low, out_high, out_low,
    out_all, attended, frame_parts, frame_recv, att_parts, att_recv,
    frames_sum, att_sum, frames_full, att_full, merged,
    row_part, row_out, states, kv_all, g_att, upd_part, upd_recv, upd_all,
    out_sems, out_a, out_b, fs_sems, fz_sems, as_sems, az_sems, ra_sems, rb_sems,
    kv_a, kv_b, up_sems, ug_a, ug_b,
):
    me = lax.axis_index("head")
    ctx = lax.axis_index("ctx")
    tokens, width = frames.shape
    local = fq.shape[1]
    heads = local // HEAD_DIM
    rows = tokens // 4
    head_rows = tokens // n
    share = local // m
    frame_count = tokens // PATCHES
    mate = ctx + 1 - 2 * lax.rem(ctx, 2)
    pending = []

    def to(axis, target, src, dst, sems, i):
        copy = pltpu.make_async_remote_copy(
            src_ref=src, dst_ref=dst, send_sem=sems.at[0, i], recv_sem=sems.at[1, i],
            device_id={axis: target}, device_id_type=MESH,
        )
        copy.start()
        pending.append(copy)
        return copy

    def columns(i):
        return pl.ds(pl.multiple_of(i * local, local), local)

    def block_rows(i, size):
        return pl.ds(pl.multiple_of(i * size, size), size)

    def peer(base, shift, size):
        return lax.rem(base + shift, size)

    def arrive(copies):
        for copy in copies:
            copy.wait_recv()

    def gather_first(buf, sems):
        return [
            to("ctx", peer(ctx, s, m), buf.at[ctx], buf.at[ctx], sems, s // 2)
            for s in range(2, m, 2)
        ]

    def gather_second(buf, sems):
        return [
            to("ctx", mate, buf.at[peer(ctx, s, m)], buf.at[peer(ctx, s, m)], sems, s // 2)
            for s in range(0, m, 2)
        ]

    barrier = pltpu.get_barrier_semaphore()
    for s in range(1, n):
        pl.semaphore_signal(
            barrier, inc=1, device_id={"head": peer(me, s, n)}, device_id_type=MESH
        )
    for s in range(1, m):
        pl.semaphore_signal(
            barrier, inc=1, device_id={"ctx": peer(ctx, s, m)}, device_id_type=MESH
        )
    pl.semaphore_wait(barrier, n - 1 + m - 1)

    own_share = fo.at[block_rows(ctx, share), :]
    out_copies = [
        to("head", peer(me, s, n), own_share, out_all.at[ctx, me], out_sems, s)
        for s in range(1, n)
    ]
    out_all[ctx, me] = fo[block_rows(ctx, share), :]

    def one_hot(owner):
        ids = owner * rows + lax.broadcasted_iota(jnp.int32, (rows, tokens), 0)
        return ids == index_row[...]

    source = split(frames[:, columns(me)])
    frame_copies = []
    for s in [*range(1, m), 0]:
        hot = one_hot(peer(ctx, s, m)).astype(jnp.float32)
        table = hot.astype(jnp.bfloat16)
        frame_parts[s, :, :local] = dot(table, source[0]) + dot(table, source[1])
        frame_parts[s, :, local:] = jnp.broadcast_to(
            jnp.sum(hot, axis=1, keepdims=True), (rows, 128)
        )
        if s:
            frame_copies.append(
                to("ctx", peer(ctx, s, m), frame_parts.at[s], frame_recv.at[s], fs_sems, s)
            )

    for i, ref in enumerate((fq, fk, fv)):
        high, low = split(ref[...])
        fw_high[:, i * local : (i + 1) * local] = high
        fw_low[:, i * local : (i + 1) * local] = low

    def one_frame(f, carry):
        here = pl.ds(pl.multiple_of(f * PATCHES, PATCHES), PATCHES)
        normed = split(layer_norm(frames[here, :]))
        qkv = dot3(normed, (fw_high[...], fw_low[...]))
        for h in range(heads):
            at = h * HEAD_DIM
            attended[here, at : at + HEAD_DIM] = attend(
                qkv[:, at : at + HEAD_DIM],
                qkv[:, local + at : local + at + HEAD_DIM],
                qkv[:, 2 * local + at : 2 * local + at + HEAD_DIM],
            )
        return carry

    half = frame_count // 2
    lax.fori_loop(0, half, one_frame, 0)
    arrive(frame_copies)
    total = frame_parts[0]
    for s in range(1, m):
        total += frame_recv[s]
    counts = total[:, local : local + 1]
    frames_sum[...] = total[:, :local] / counts
    frames_full[:, columns(me)] = frames_sum[...]
    sum_copies = [
        to("head", peer(me, s, n), frames_sum, frames_full.at[:, columns(me)], fz_sems, s)
        for s in range(1, n)
    ]
    lax.fori_loop(half, frame_count, one_frame, 0)

    source = split(attended[...])
    att_copies = []
    for s in [*range(1, m), 0]:
        table = one_hot(peer(ctx, s, m)).astype(jnp.float32).astype(jnp.bfloat16)
        att_parts[s] = dot(table, source[0]) + dot(table, source[1])
        if s:
            att_copies.append(
                to("ctx", peer(ctx, s, m), att_parts.at[s], att_recv.at[s], as_sems, s)
            )
    for i, ref in enumerate((gq, gk, gv)):
        high, low = split(ref[...])
        gw_high[:, i * local : (i + 1) * local] = high
        gw_low[:, i * local : (i + 1) * local] = low
    arrive(out_copies)
    out_copies = gather_first(out_all, out_a)
    arrive(att_copies)
    total = att_parts[0]
    for s in range(1, m):
        total += att_recv[s]
    att_sum[...] = total / counts
    att_full[:, columns(me)] = att_sum[...]
    att_copies = [
        to("head", peer(me, s, n), att_sum, att_full.at[:, columns(me)], az_sems, s)
        for s in range(1, n)
    ]

    row_copies = [
        to(
            "head", peer(me, s, n), attended.at[block_rows(peer(me, s, n), head_rows), :],
            row_part.at[:, columns(me)], ra_sems, s,
        )
        for s in range(1, n)
    ]
    row_part[:, columns(me)] = attended[block_rows(me, head_rows), :]

    arrive(out_copies)
    out_copies = gather_second(out_all, out_b)
    arrive(out_copies)
    for i in range(n):
        high, low = split(out_all[:, i].reshape(local, width))
        out_high[i * local : (i + 1) * local, :] = high
        out_low[i * local : (i + 1) * local, :] = low
    projection = (out_high, out_low)

    arrive(sum_copies)
    arrive(att_copies)
    full = frames_full[...] + dot3(
        split(att_full[...]), (projection[0][...], projection[1][...])
    )
    att_full[...] = full
    merged[...] = att_full[:, columns(me)]
    normed = split(layer_norm(full))
    kv_all[ctx] = dot3(normed, (gw_high[:, local:], gw_low[:, local:]))
    kv_copies = gather_first(kv_all, kv_a)
    query = dot3(normed, (gw_high[:, :local], gw_low[:, :local]))
    go_pair = split(go[...])
    arrive(kv_copies)
    kv_copies = gather_second(kv_all, kv_b)

    arrive(row_copies)
    row_out[...] = dot3(split(row_part[...]), (projection[0][...], projection[1][...]))
    back_copies = [
        to(
            "head", peer(me, s, n), row_out.at[:, columns(peer(me, s, n))],
            states.at[block_rows(me, head_rows), :], rb_sems, s,
        )
        for s in range(1, n)
    ]
    states[block_rows(me, head_rows), :] = row_out[:, columns(me)]

    arrive(kv_copies)
    for h in range(heads):
        at = h * HEAD_DIM
        g_att[:, at : at + HEAD_DIM] = attend(
            query[:, at : at + HEAD_DIM],
            kv_all[:, :, at : at + HEAD_DIM].reshape(m * rows, HEAD_DIM),
            kv_all[:, :, local + at : local + at + HEAD_DIM].reshape(m * rows, HEAD_DIM),
        )
    upd_part[...] = dot3(split(g_att[...]), go_pair)
    upd_copies = [
        to(
            "head", peer(me, s, n), upd_part.at[:, columns(peer(me, s, n))],
            upd_recv.at[s], up_sems, s,
        )
        for s in range(1, n)
    ]
    update = upd_part[:, columns(me)]
    arrive(upd_copies)
    for s in range(1, n):
        update += upd_recv[s]
    upd_all[ctx] = update
    upd_copies = gather_first(upd_all, ug_a)
    merged_tokens[...] = merged[...] + update
    arrive(upd_copies)
    upd_copies = gather_second(upd_all, ug_b)
    arrive(back_copies)
    arrive(upd_copies)
    source = split(upd_all[...].reshape(m * rows, local))

    def spread(f, carry):
        here = pl.ds(pl.multiple_of(f * PATCHES, PATCHES), PATCHES)
        ids = lax.broadcasted_iota(jnp.int32, (PATCHES, m * rows), 1)
        table = (ids == index_col[here, :]).astype(jnp.float32).astype(jnp.bfloat16)
        refined[here, :] = (
            frames[here, columns(me)]
            + states[here, :]
            + (dot(table, source[0]) + dot(table, source[1]))
        )
        return carry

    lax.fori_loop(0, frame_count, spread, 0)
    for copy in pending:
        copy.wait_send()


def per_device(frames_in, merge_index, *weights):
    n = lax.axis_size("head")
    m = lax.axis_size("ctx")
    tokens, width = frames_in.shape
    local = weights[0].shape[1]
    rows = tokens // 4
    head_rows = tokens // n
    share = local // m
    f32, bf16 = jnp.float32, jnp.bfloat16

    def sems(count):
        return pltpu.SemaphoreType.DMA((2, count))

    scratch = [
        pltpu.VMEM((width, 3 * local), bf16),
        pltpu.VMEM((width, 3 * local), bf16),
        pltpu.VMEM((width, 3 * local), bf16),
        pltpu.VMEM((width, 3 * local), bf16),
        pltpu.VMEM((n * local, width), bf16),
        pltpu.VMEM((n * local, width), bf16),
        pltpu.VMEM((m, n, share, width), f32),
        pltpu.VMEM((tokens, local), f32),
        pltpu.VMEM((m, rows, local + 128), f32),
        pltpu.VMEM((m, rows, local + 128), f32),
        pltpu.VMEM((m, rows, local), f32),
        pltpu.VMEM((m, rows, local), f32),
        pltpu.VMEM((rows, local), f32),
        pltpu.VMEM((rows, local), f32),
        pltpu.VMEM((rows, width), f32),
        pltpu.VMEM((rows, width), f32),
        pltpu.VMEM((rows, local), f32),
        pltpu.VMEM((head_rows, width), f32),
        pltpu.VMEM((head_rows, width), f32),
        pltpu.VMEM((tokens, local), f32),
        pltpu.VMEM((m, rows, 2 * local), f32),
        pltpu.VMEM((rows, local), f32),
        pltpu.VMEM((rows, width), f32),
        pltpu.VMEM((n, rows, local), f32),
        pltpu.VMEM((m, rows, local), f32),
        sems(n), sems(m), sems(m), sems(m), sems(n), sems(m), sems(n), sems(n), sems(n),
        sems(m), sems(m), sems(n), sems(m), sems(m),
    ]
    vmem = pl.BlockSpec(memory_space=pltpu.VMEM)
    return pl.pallas_call(
        functools.partial(kernel, n, m),
        out_shape=(
            jax.ShapeDtypeStruct((tokens, local), f32),
            jax.ShapeDtypeStruct((rows, local), f32),
        ),
        in_specs=[vmem] * (3 + len(weights)),
        out_specs=(vmem, vmem),
        scratch_shapes=scratch,
        compiler_params=pltpu.CompilerParams(
            collective_id=0, has_side_effects=True, vmem_limit_bytes=60 * 1024 * 1024
        ),
    )(frames_in, merge_index.reshape(1, tokens), merge_index.reshape(tokens, 1), *weights)


def solution(mesh):
    placed = (
        P(("scene", "ctx"), None),
        P(("scene", "ctx")),
        P(None, "head"),
        P(None, "head"),
        P(None, "head"),
        P("head", None),
        P(None, "head"),
        P(None, "head"),
        P(None, "head"),
        P("head", None),
    )
    return jax.shard_map(
        per_device,
        mesh=mesh,
        in_specs=placed,
        out_specs=(P(("scene", "ctx"), "head"), P(("scene", "ctx"), "head")),
        check_vma=False,
    )
```

```python
import functools

import jax
import jax.numpy as jnp
from jax import lax
from jax.experimental import pallas as pl
from jax.experimental.pallas import tpu as pltpu
from jax.sharding import PartitionSpec as P

HEAD_DIM = 64
PATCHES = 256
MESH = pl.DeviceIdType.MESH


def split(x):
    high = x.astype(jnp.bfloat16)
    return high, (x - high.astype(jnp.float32)).astype(jnp.bfloat16)


def dot(a, b, contract=((1,), (0,))):
    return lax.dot_general(a, b, (contract, ((), ())), preferred_element_type=jnp.float32)


def dot3(a, b, contract=((1,), (0,))):
    (a_high, a_low), (b_high, b_low) = a, b
    return (
        dot(a_high, b_high, contract) + dot(a_high, b_low, contract) + dot(a_low, b_high, contract)
    )


def layer_norm(entries):
    center = entries - jnp.mean(entries, axis=-1, keepdims=True)
    spread = jnp.mean(center * center, axis=-1, keepdims=True)
    return center * lax.rsqrt(spread + 1e-06)


def attend(query, key, value):
    scores = dot3(split(query * HEAD_DIM ** (-0.5)), split(key), ((1,), (1,)))
    weights = jnp.exp(scores - jnp.max(scores, axis=-1, keepdims=True))
    total = jnp.sum(weights, axis=-1, keepdims=True)
    return dot3(split(weights), split(value)) / total


def kernel(
    n, m,
    frames, index_row, index_col, fq, fk, fv, fo, gq, gk, gv, go,
    refined, merged_tokens,
    fw_high, fw_low, gw_high, gw_low, out_high, out_low,
    out_all, attended, frame_parts, frame_recv, att_parts, att_recv,
    frames_sum, att_sum, frames_full, att_full, merged,
    row_part, row_out, states, kv_all, g_att, upd_part, upd_recv, upd_all,
    out_sems, out_a, out_b, fs_sems, fz_sems, as_sems, az_sems, ra_sems, rb_sems,
    kv_a, kv_b, up_sems, ug_a, ug_b,
):
    me = lax.axis_index("head")
    ctx = lax.axis_index("ctx")
    tokens, width = frames.shape
    local = fq.shape[1]
    heads = local // HEAD_DIM
    rows = tokens // 4
    head_rows = tokens // n
    share = local // m
    frame_count = tokens // PATCHES
    mate = ctx + 1 - 2 * lax.rem(ctx, 2)
    pending = []

    def to(axis, target, src, dst, sems, i):
        copy = pltpu.make_async_remote_copy(
            src_ref=src, dst_ref=dst, send_sem=sems.at[0, i], recv_sem=sems.at[1, i],
            device_id={axis: target}, device_id_type=MESH,
        )
        copy.start()
        pending.append(copy)
        return copy

    def columns(i):
        return pl.ds(pl.multiple_of(i * local, local), local)

    def block_rows(i, size):
        return pl.ds(pl.multiple_of(i * size, size), size)

    def peer(base, shift, size):
        return lax.rem(base + shift, size)

    def arrive(copies):
        for copy in copies:
            copy.wait_recv()

    def gather_first(buf, sems, mate_sems):
        far = [
            to("ctx", peer(ctx, s, m), buf.at[ctx], buf.at[ctx], sems, s // 2)
            for s in range(2, m, 2)
        ]
        return far, [to("ctx", mate, buf.at[ctx], buf.at[ctx], mate_sems, 0)]

    def gather_second(buf, copies, mate_sems):
        far, near = copies
        for i, s in enumerate(range(2, m, 2)):
            far[i].wait_recv()
            source = buf.at[peer(ctx, m - s, m)]
            near.append(to("ctx", mate, source, source, mate_sems, i + 1))
        return near

    barrier = pltpu.get_barrier_semaphore()
    for s in range(1, n):
        pl.semaphore_signal(
            barrier, inc=1, device_id={"head": peer(me, s, n)}, device_id_type=MESH
        )
    for s in range(1, m):
        pl.semaphore_signal(
            barrier, inc=1, device_id={"ctx": peer(ctx, s, m)}, device_id_type=MESH
        )
    pl.semaphore_wait(barrier, n - 1 + m - 1)

    own_share = fo.at[block_rows(ctx, share), :]
    out_copies = [
        to("head", peer(me, s, n), own_share, out_all.at[ctx, me], out_sems, s)
        for s in range(1, n)
    ]
    out_all[ctx, me] = fo[block_rows(ctx, share), :]

    def one_hot(owner):
        ids = owner * rows + lax.broadcasted_iota(jnp.int32, (rows, tokens), 0)
        return ids == index_row[...]

    source = split(frames[:, columns(me)])
    frame_copies = []
    for s in [*range(1, m), 0]:
        hot = one_hot(peer(ctx, s, m)).astype(jnp.float32)
        table = hot.astype(jnp.bfloat16)
        frame_parts[s, :, :local] = dot(table, source[0]) + dot(table, source[1])
        frame_parts[s, :, local:] = jnp.broadcast_to(
            jnp.sum(hot, axis=1, keepdims=True), (rows, 128)
        )
        if s:
            frame_copies.append(
                to("ctx", peer(ctx, s, m), frame_parts.at[s], frame_recv.at[s], fs_sems, s)
            )

    for i, ref in enumerate((fq, fk, fv)):
        high, low = split(ref[...])
        fw_high[:, i * local : (i + 1) * local] = high
        fw_low[:, i * local : (i + 1) * local] = low

    def one_frame(f, carry):
        here = pl.ds(pl.multiple_of(f * PATCHES, PATCHES), PATCHES)
        normed = split(layer_norm(frames[here, :]))
        qkv = dot3(normed, (fw_high[...], fw_low[...]))
        for h in range(heads):
            at = h * HEAD_DIM
            attended[here, at : at + HEAD_DIM] = attend(
                qkv[:, at : at + HEAD_DIM],
                qkv[:, local + at : local + at + HEAD_DIM],
                qkv[:, 2 * local + at : 2 * local + at + HEAD_DIM],
            )
        return carry

    half = frame_count // 2
    lax.fori_loop(0, half, one_frame, 0)
    arrive(frame_copies)
    total = frame_parts[0]
    for s in range(1, m):
        total += frame_recv[s]
    counts = total[:, local : local + 1]
    frames_sum[...] = total[:, :local] / counts
    frames_full[:, columns(me)] = frames_sum[...]
    sum_copies = [
        to("head", peer(me, s, n), frames_sum, frames_full.at[:, columns(me)], fz_sems, s)
        for s in range(1, n)
    ]
    lax.fori_loop(half, frame_count, one_frame, 0)

    row_copies = [
        to(
            "head", peer(me, s, n), attended.at[block_rows(peer(me, s, n), head_rows), :],
            row_part.at[:, columns(me)], ra_sems, s,
        )
        for s in range(1, n)
    ]
    row_part[:, columns(me)] = attended[block_rows(me, head_rows), :]

    source = split(attended[...])
    att_copies = []
    for s in [*range(1, m), 0]:
        table = one_hot(peer(ctx, s, m)).astype(jnp.float32).astype(jnp.bfloat16)
        att_parts[s] = dot(table, source[0]) + dot(table, source[1])
        if s:
            att_copies.append(
                to("ctx", peer(ctx, s, m), att_parts.at[s], att_recv.at[s], as_sems, s)
            )
    for i, ref in enumerate((gq, gk, gv)):
        high, low = split(ref[...])
        gw_high[:, i * local : (i + 1) * local] = high
        gw_low[:, i * local : (i + 1) * local] = low
    arrive(out_copies)
    out_copies = gather_first(out_all, out_a, out_b)
    arrive(att_copies)
    total = att_parts[0]
    for s in range(1, m):
        total += att_recv[s]
    att_sum[...] = total / counts
    att_full[:, columns(me)] = att_sum[...]
    att_copies = [
        to("head", peer(me, s, n), att_sum, att_full.at[:, columns(me)], az_sems, s)
        for s in range(1, n)
    ]

    out_copies = gather_second(out_all, out_copies, out_b)
    arrive(out_copies)
    for i in range(n):
        high, low = split(out_all[:, i].reshape(local, width))
        out_high[i * local : (i + 1) * local, :] = high
        out_low[i * local : (i + 1) * local, :] = low
    projection = (out_high, out_low)

    arrive(sum_copies)
    arrive(att_copies)
    full = frames_full[...] + dot3(
        split(att_full[...]), (projection[0][...], projection[1][...])
    )
    att_full[...] = full
    merged[...] = att_full[:, columns(me)]
    normed = split(layer_norm(full))
    kv_all[ctx] = dot3(normed, (gw_high[:, local:], gw_low[:, local:]))
    kv_copies = gather_first(kv_all, kv_a, kv_b)
    arrive(row_copies)
    row_out[...] = dot3(split(row_part[...]), (projection[0][...], projection[1][...]))
    back_copies = [
        to(
            "head", peer(me, s, n), row_out.at[:, columns(peer(me, s, n))],
            states.at[block_rows(me, head_rows), :], rb_sems, s,
        )
        for s in range(1, n)
    ]
    states[block_rows(me, head_rows), :] = row_out[:, columns(me)]
    query = dot3(normed, (gw_high[:, :local], gw_low[:, :local]))
    go_pair = split(go[...])
    kv_copies = gather_second(kv_all, kv_copies, kv_b)

    arrive(kv_copies)
    part = rows // 2
    halves = []
    for half in range(2):
        here = slice(half * part, (half + 1) * part)
        for h in range(heads):
            at = h * HEAD_DIM
            g_att[here, at : at + HEAD_DIM] = attend(
                query[here, at : at + HEAD_DIM],
                kv_all[:, :, at : at + HEAD_DIM].reshape(m * rows, HEAD_DIM),
                kv_all[:, :, local + at : local + at + HEAD_DIM].reshape(m * rows, HEAD_DIM),
            )
        upd_part[here, :] = dot3(split(g_att[here, :]), go_pair)
        halves.append([
            to(
                "head", peer(me, s, n),
                upd_part.at[pl.ds(half * part, part), columns(peer(me, s, n))],
                upd_recv.at[s, pl.ds(half * part, part)], up_sems, half * n + s,
            )
            for s in range(1, n)
        ])
    firsts = []
    for half in range(2):
        here = pl.ds(half * part, part)
        arrive(halves[half])
        update = upd_part[here, columns(me)]
        for s in range(1, n):
            update += upd_recv[s, here]
        upd_all[ctx, here] = update
        own = upd_all.at[ctx, here]
        merged_tokens[here, :] = merged[here, :] + update
        far = [
            to("ctx", peer(ctx, s, m), own, own, ug_a, half * m + s // 2) for s in range(2, m, 2)
        ]
        firsts.append((far, [to("ctx", mate, own, own, ug_b, half * m)]))
    for half in range(2):
        here = pl.ds(half * part, part)
        far, near = firsts[half]
        for i, s in enumerate(range(2, m, 2)):
            far[i].wait_recv()
            block = upd_all.at[peer(ctx, m - s, m), here]
            near.append(to("ctx", mate, block, block, ug_b, half * m + i + 1))
    arrive(back_copies)
    arrive(firsts[0][1])
    arrive(firsts[1][1])
    source = split(upd_all[...].reshape(m * rows, local))

    def spread(f, carry):
        here = pl.ds(pl.multiple_of(f * PATCHES, PATCHES), PATCHES)
        ids = lax.broadcasted_iota(jnp.int32, (PATCHES, m * rows), 1)
        table = (ids == index_col[here, :]).astype(jnp.float32).astype(jnp.bfloat16)
        refined[here, :] = (
            frames[here, columns(me)]
            + states[here, :]
            + (dot(table, source[0]) + dot(table, source[1]))
        )
        return carry

    lax.fori_loop(0, frame_count, spread, 0)
    for copy in pending:
        copy.wait_send()


def per_device(frames_in, merge_index, *weights):
    n = lax.axis_size("head")
    m = lax.axis_size("ctx")
    tokens, width = frames_in.shape
    local = weights[0].shape[1]
    rows = tokens // 4
    head_rows = tokens // n
    share = local // m
    f32, bf16 = jnp.float32, jnp.bfloat16

    def sems(count):
        return pltpu.SemaphoreType.DMA((2, count))

    scratch = [
        pltpu.VMEM((width, 3 * local), bf16),
        pltpu.VMEM((width, 3 * local), bf16),
        pltpu.VMEM((width, 3 * local), bf16),
        pltpu.VMEM((width, 3 * local), bf16),
        pltpu.VMEM((n * local, width), bf16),
        pltpu.VMEM((n * local, width), bf16),
        pltpu.VMEM((m, n, share, width), f32),
        pltpu.VMEM((tokens, local), f32),
        pltpu.VMEM((m, rows, local + 128), f32),
        pltpu.VMEM((m, rows, local + 128), f32),
        pltpu.VMEM((m, rows, local), f32),
        pltpu.VMEM((m, rows, local), f32),
        pltpu.VMEM((rows, local), f32),
        pltpu.VMEM((rows, local), f32),
        pltpu.VMEM((rows, width), f32),
        pltpu.VMEM((rows, width), f32),
        pltpu.VMEM((rows, local), f32),
        pltpu.VMEM((head_rows, width), f32),
        pltpu.VMEM((head_rows, width), f32),
        pltpu.VMEM((tokens, local), f32),
        pltpu.VMEM((m, rows, 2 * local), f32),
        pltpu.VMEM((rows, local), f32),
        pltpu.VMEM((rows, width), f32),
        pltpu.VMEM((n, rows, local), f32),
        pltpu.VMEM((m, rows, local), f32),
        sems(n), sems(m), sems(m), sems(m), sems(n), sems(m), sems(n), sems(n), sems(n),
        sems(m), sems(m), sems(2 * n), sems(2 * m), sems(2 * m),
    ]
    vmem = pl.BlockSpec(memory_space=pltpu.VMEM)
    return pl.pallas_call(
        functools.partial(kernel, n, m),
        out_shape=(
            jax.ShapeDtypeStruct((tokens, local), f32),
            jax.ShapeDtypeStruct((rows, local), f32),
        ),
        in_specs=[vmem] * (3 + len(weights)),
        out_specs=(vmem, vmem),
        scratch_shapes=scratch,
        compiler_params=pltpu.CompilerParams(
            collective_id=0, has_side_effects=True, vmem_limit_bytes=60 * 1024 * 1024
        ),
    )(frames_in, merge_index.reshape(1, tokens), merge_index.reshape(tokens, 1), *weights)


def solution(mesh):
    placed = (
        P(("scene", "ctx"), None),
        P(("scene", "ctx")),
        P(None, "head"),
        P(None, "head"),
        P(None, "head"),
        P("head", None),
        P(None, "head"),
        P(None, "head"),
        P(None, "head"),
        P("head", None),
    )
    return jax.shard_map(
        per_device,
        mesh=mesh,
        in_specs=placed,
        out_specs=(P(("scene", "ctx"), "head"), P(("scene", "ctx"), "head")),
        check_vma=False,
    )
```
